32 devices in a mesh: groups: 2 (over y), ctx: 4 (over z), head: 2 (over x), rows: 2 (over core).
Axes of the slice: x: 2, y: 2, z: 4, core: 2. Of those that a mesh axis runs over, the one named last changes fastest.
Arguments:
- keys: bfloat16 [65536, 1024], P(('groups', 'ctx'), 'head'), parts along dimension 0, may hold values from -18 to 18
- values: bfloat16 [65536, 1024], P(('groups', 'ctx'), 'head'), parts along dimension 0, may hold values from -6 to 6
- window_q: bfloat16 [64, 8192], P(('groups', 'ctx'), 'head'), parts along dimension 0, may hold values from -6 to 6
- keep_stretches: int32 [16, 20], P(('groups', 'head')), parts along dimension 0, may hold values from 0 to 62, as said below
- dec_q: bfloat16 [128, 4, 8192], P('groups', None, 'head'), parts along dimension 0, may hold values from -6 to 6
- dec_k: bfloat16 [128, 4, 1024], P('groups', None, 'head'), parts along dimension 0, may hold values from -8 to 8
- dec_v: bfloat16 [128, 4, 1024], P('groups', None, 'head'), parts along dimension 0, may hold values from -6 to 6
- row_order: int32 [128], P('groups'), parts along dimension 0, may hold values from 0 to 63, each once
Outputs:
- stretch_scores: float32 [16, 64], P(('groups', 'head', 'rows'), 'ctx'), parts along dimension 0
- decoded: bfloat16 [128, 4, 8192], P(('groups', 'ctx', 'rows'), None, 'head'), parts along dimension 0
The draws below stay inside these ranges and needn't reach their ends.
There are 2 independent parts, one for each index of `groups`. The reference program is written for one: setup_inputs(seed, part) draws one part's arguments, and reference() takes and returns one part's arrays. A program takes and returns all parts, laid end to end along the dimension named above; each array names one. Nothing has to cross between parts.
Inputs may be any that keep to these rules, and one draw needn't show every extreme that they name: keep_stretches[k] lists 20 distinct stretch numbers of key-value head k in ascending order and never the last stretch; for every head some context shard has all 16 of its stretches listed.
All inputs are finite; a program needn't handle non-finite values.
Results may differ from the reference program's by a relative error of at most 0.0045.
Values may be sent and summed in bfloat16 or wider, within the bound.
A program may use at most 128 MiB of HBM per device.

```python
import jax
import jax.numpy as jnp
from jax import lax

QH = 64
KVH = 8
HD = 128
STRETCH = 512
W = 32
ROWS = 64
STEPS = 4
CTX = 32768
CPD = 16
NCHUNK = 64
KEEP = 20
N_CTX = 4


def own_affinity():
    return (jnp.log(jnp.float32(KEEP * STRETCH + W)) + 4.0) / HD ** 0.5


def draw_keys(key, part):
    sample = 3.0 * jnp.clip(jax.random.normal(jax.random.fold_in(key, 1), (CTX, KVH * HD)), -6.0, 6.0)
    return sample.astype(jnp.bfloat16)


def draw_window_q(key, part):
    sample = jnp.clip(jax.random.normal(jax.random.fold_in(key, 21), (W, QH * HD)), -6.0, 6.0)
    return sample.astype(jnp.bfloat16)


def decode_common(key):
    shape = (ROWS, STEPS, KVH, HD)
    common = jnp.clip(jax.random.normal(jax.random.fold_in(key, 31), shape), -3.0, 3.0)
    return common


def draw_dec_q(key, part):
    common = decode_common(key)
    shape = (ROWS, STEPS, KVH, QH // KVH, HD)
    jitter = jax.random.normal(jax.random.fold_in(key, 35), shape)
    sample = jnp.clip(common[:, :, :, None, :] + 0.6 * jitter, -6.0, 6.0).reshape(ROWS, STEPS, QH * HD)
    return sample.astype(jnp.bfloat16)


def draw_dec_k(key, part):
    common = decode_common(key)
    shape = (ROWS, STEPS, KVH, HD)
    jitter = jax.random.normal(jax.random.fold_in(key, 36), shape)
    sample = jnp.clip(own_affinity() * common + 0.5 * jitter, -8.0, 8.0).reshape(ROWS, STEPS, KVH * HD)
    return sample.astype(jnp.bfloat16)


def draw_keep_stretches(key, part):
    full_shard = jax.random.randint(jax.random.fold_in(key, 301), (KVH,), 0, N_CTX - 1)
    levels = jax.random.randint(jax.random.fold_in(key, 302), (KVH, N_CTX), 0, 4)
    jitter = jax.random.randint(jax.random.fold_in(key, 303), (KVH, NCHUNK), 0, 1024)
    stretch_ids = jnp.arange(NCHUNK, dtype=jnp.int32)
    shard_ids = stretch_ids // CPD
    ranking = jitter + 1024 * levels[:, shard_ids]
    ranking = jnp.where(shard_ids[None, :] == full_shard[:, None], 1 << 20, ranking)
    ranking = jnp.where(stretch_ids[None, :] == NCHUNK - 1, -1, ranking)
    ranking = ranking * NCHUNK + stretch_ids[None, :]
    unused, chosen = lax.top_k(ranking, KEEP)
    return jnp.sort(chosen.astype(jnp.int32), axis=1)


def steps_of(key, extent, shards, low, largest):
    loudness, own = 1.0, jax.random.fold_in(key, 6)
    for axis_at, parts in shards:
        draws = jnp.exp(jax.random.uniform(jax.random.fold_in(own, axis_at), (parts,), jnp.float32, low / len(shards), largest / len(shards)))
        loudness = loudness * jnp.repeat(draws, extent[axis_at] // parts).reshape([-1 if axis == axis_at else 1 for axis in range(len(extent))])
    return loudness


def noise(rng, shape, scale, bound, shards=(), kind=jnp.bfloat16):
    level = steps_of(rng, shape, shards, -0.22, 0.18) if shards else 1.0
    drawn = jax.random.normal(rng, shape, jnp.float32) * scale * level
    return jnp.minimum(jnp.maximum(drawn, -bound), bound).astype(kind)


def setup_inputs(seed: int = 0, part: int = 0) -> dict:
    key_list = jax.random.split(jax.random.key(seed), 9)
    part_splits = jax.random.split(jax.random.fold_in(key_list[8], part), 9)
    keys = draw_keys(jax.random.fold_in(jax.random.fold_in(key_list[8], part), 71), part)
    values = noise(part_splits[1], (CTX, KVH * HD), 1.0, 6.0, ((0, 4), (1, 2)))
    window_q = draw_window_q(jax.random.fold_in(jax.random.fold_in(key_list[8], part), 71), part)
    keep_stretches = draw_keep_stretches(jax.random.fold_in(jax.random.fold_in(key_list[8], part), 71), part)
    dec_q = draw_dec_q(jax.random.fold_in(jax.random.fold_in(key_list[8], part), 71), part)
    dec_k = draw_dec_k(jax.random.fold_in(jax.random.fold_in(key_list[8], part), 71), part)
    dec_v = noise(part_splits[6], (ROWS, STEPS, KVH * HD), 1.0, 6.0, ((2, 2),))
    row_order = jax.random.permutation(part_splits[7], ROWS).astype(jnp.int32)
    return {"keys": keys, "values": values, "window_q": window_q, "keep_stretches": keep_stretches, "dec_q": dec_q, "dec_k": dec_k, "dec_v": dec_v, "row_order": row_order}


MASK_FILL = -1.0e30


def score_head(inputs):
    window_query, head_keys = inputs
    scores = jnp.einsum("whd,td->wht", window_query.astype(jnp.float32), head_keys.astype(jnp.float32)) * (HD ** -0.5)
    positions = jnp.arange(CTX, dtype=jnp.int32)
    reaches = CTX - W + jnp.arange(W, dtype=jnp.int32)
    allowed = (positions[None, :] <= reaches[:, None])[:, None, :]
    masked = jnp.where(allowed, scores, MASK_FILL)
    maxima = jnp.max(masked, axis=2, keepdims=True)
    weights = jnp.where(allowed, jnp.exp(masked - maxima), 0.0)
    probability = weights / jnp.sum(weights, axis=2, keepdims=True)
    return jnp.sum(probability, axis=(0, 1)).reshape(NCHUNK, STRETCH).sum(axis=1)


def decode_head(inputs):
    head_query, head_keys, head_values, keep_list, own_keys, own_values = inputs
    positions = (keep_list[:, None] * STRETCH + jnp.arange(STRETCH, dtype=jnp.int32)[None, :]).reshape(-1)
    positions = jnp.concatenate([positions.astype(jnp.int32), jnp.arange(CTX - W, CTX, dtype=jnp.int32)])
    kept_keys = head_keys[positions]
    kept_values = head_values[positions]
    causal = (jnp.arange(STEPS, dtype=jnp.int32)[None, :] <= jnp.arange(STEPS, dtype=jnp.int32)[:, None])[None, :, None, :]

    def one_block(block_data):
        queries, self_keys, self_values = block_data
        rows_block = queries.shape[0]
        group_size = queries.shape[2]
        flat_query = queries.reshape(-1, HD)
        ctx_scores = jnp.dot(flat_query, kept_keys.T, preferred_element_type=jnp.float32) * (HD ** -0.5)
        own_scores = jnp.einsum("rshd,rtd->rsht", queries.astype(jnp.float32), self_keys.astype(jnp.float32)) * (HD ** -0.5)
        own_masked = jnp.where(causal, own_scores, MASK_FILL)
        maxima = jnp.maximum(jnp.max(ctx_scores, axis=1), jnp.max(own_masked.reshape(-1, STEPS), axis=1))
        ctx_weights = jnp.exp(ctx_scores - maxima[:, None])
        own_weights = jnp.where(causal, jnp.exp(own_masked - maxima.reshape(rows_block, STEPS, group_size, 1)), 0.0)
        totals = jnp.sum(ctx_weights, axis=1) + jnp.sum(own_weights.reshape(-1, STEPS), axis=1)
        own_rounded = lax.optimization_barrier(own_weights.astype(jnp.bfloat16)).astype(jnp.float32)
        weighted = jnp.dot(ctx_weights.astype(jnp.bfloat16), kept_values, preferred_element_type=jnp.float32)
        weighted = weighted + jnp.einsum("rsht,rtd->rshd", own_rounded, self_values.astype(jnp.float32)).reshape(-1, HD)
        return (weighted / totals[:, None]).reshape(rows_block, STEPS, group_size, HD)

    group_size = head_query.shape[2]
    outputs = lax.map(one_block, (head_query.reshape(ROWS // 8, 8, STEPS, group_size, HD), own_keys.reshape(ROWS // 8, 8, STEPS, HD), own_values.reshape(ROWS // 8, 8, STEPS, HD)))
    return outputs.reshape(ROWS, STEPS, group_size, HD)


def reference(keys, values, window_q, keep_stretches, dec_q, dec_k, dec_v, row_order):
    group_size = QH // KVH
    key_heads = keys.reshape(CTX, KVH, HD).transpose(1, 0, 2)
    value_heads = values.reshape(CTX, KVH, HD).transpose(1, 0, 2)
    query_heads = window_q.reshape(W, KVH, group_size, HD).transpose(1, 0, 2, 3)
    stretch_scores = lax.map(score_head, (query_heads, key_heads))
    decode_query = dec_q.reshape(ROWS, STEPS, KVH, group_size, HD).transpose(2, 0, 1, 3, 4)
    own_keys = dec_k.reshape(ROWS, STEPS, KVH, HD).transpose(2, 0, 1, 3)
    own_values = dec_v.reshape(ROWS, STEPS, KVH, HD).transpose(2, 0, 1, 3)
    outputs = lax.map(decode_head, (decode_query, key_heads, value_heads, keep_stretches, own_keys, own_values))
    outputs = outputs.transpose(1, 2, 0, 3, 4).reshape(ROWS, STEPS, QH * HD)
    decoded = outputs[row_order.astype(jnp.int32)].astype(jnp.bfloat16)
    return stretch_scores, decoded
```

```python
import functools
import math

import jax
import jax.numpy as jnp
from jax import lax
from jax.experimental import pallas as pl
from jax.experimental.pallas import tpu as pltpu
from jax.sharding import PartitionSpec as P

QH = 64
KVH = 8
HD = 128
STRETCH = 512
W = 32
FILL = -1e30
SCALE = HD ** -0.5 * math.log2(math.e)
NT = (((1,), (1,)), ((), ()))
TN = (((0,), (0,)), ((), ()))
VMEM_LIMIT = 48 * 1024 * 1024


def dot(a, b, dims):
    return lax.dot_general(a, b, dims, preferred_element_type=jnp.float32)


def decode_kernel(parts, steps, meta, keep, pick, dq, dk, dv, k_ref, v_ref, out, lse, q_s, acc, m_s, l_s):
    head = pl.program_id(0)
    group = dq.shape[1] // HD
    per = pick.shape[0] // parts
    cols = group * per
    stretches = k_ref.shape[0] // STRETCH
    base = meta[0] * stretches

    gathered = dot(pick[...], dq[...], (((1,), (0,)), ((), ()))).astype(jnp.bfloat16)
    for d in range(parts):
        for g in range(group):
            q_s[pl.ds(d * cols + g * per, per), :] = gathered[d * per:(d + 1) * per, g * HD:(g + 1) * HD]
    acc[...] = jnp.zeros_like(acc)
    m_s[...] = jnp.full_like(m_s, FILL)
    l_s[...] = jnp.zeros_like(l_s)

    def update(key, value, mask=None):
        for d in range(parts):
            at = pl.ds(d * cols, cols)
            s = dot(key, q_s[at, :], NT)
            if mask is not None:
                s = jnp.where(mask(d, s.shape), s, FILL)
            m_old = m_s[:, at]
            m_new = jnp.maximum(m_old, jnp.max(s, axis=0, keepdims=True))
            p = jnp.exp2(s * SCALE - m_new * SCALE)
            shrink = jnp.exp2((m_old - m_new) * SCALE)
            m_s[:, at] = m_new
            l_s[:, at] = l_s[:, at] * shrink + jnp.sum(p, axis=0, keepdims=True)
            acc[:, at] = acc[:, at] * shrink + dot(value, p.astype(jnp.bfloat16), TN)

    def count(i, found):
        start, many = found
        stretch = keep[head, i] - base
        return (start + (stretch < 0).astype(jnp.int32),
                many + ((stretch >= 0) & (stretch < stretches)).astype(jnp.int32))

    start, many = lax.fori_loop(0, keep.shape[1], count, (jnp.int32(0), jnp.int32(0)))

    def one(i, carry):
        at = pl.ds(pl.multiple_of((keep[head, start + i] - base) * STRETCH, STRETCH), STRETCH)
        update(k_ref[at, :], v_ref[at, :])
        return carry

    lax.fori_loop(0, many, one, 0)

    @pl.when(meta[1] == 1)
    def _():
        tail = pl.ds(k_ref.shape[0] - W, W)
        update(k_ref[tail, :], v_ref[tail, :])
        own_k = dot(pick[...], dk[...], (((1,), (0,)), ((), ()))).astype(jnp.bfloat16)
        own_v = dot(pick[...], dv[...], (((1,), (0,)), ((), ()))).astype(jnp.bfloat16)
        each = per // steps

        def mask(d, shape):
            key_at = lax.broadcasted_iota(jnp.int32, shape, 0)
            query_at = lax.broadcasted_iota(jnp.int32, shape, 1) % per
            inside = key_at % per
            return ((key_at // per == d) & (inside % each == query_at % each)
                    & (inside // each <= query_at // each))

        update(own_k, own_v, mask)

    l = l_s[...]
    some = l > 0.0
    safe = jnp.where(some, l, 1.0)
    inverse = jnp.where(some, 1.0 / safe, 0.0)
    level = jnp.where(some, m_s[...] * SCALE + jnp.log2(safe), FILL)
    for d in range(parts):
        at = pl.ds(d * cols, cols)
        out[d] = (acc[:, at] * inverse[:, d * cols:(d + 1) * cols]).astype(jnp.bfloat16)
        lse[d] = level[:, d * cols:(d + 1) * cols]


def decode(meta, keep, pick, dq, dk, dv, keys, values, parts, steps):
    heads = keys.shape[1] // HD
    group = dq.shape[1] // (heads * HD)
    count = pick.shape[0] * group
    cols = count // parts
    ctx = keys.shape[0]
    column = lambda rows, width: pl.BlockSpec((rows, width), lambda h, *_: (0, h))
    return pl.pallas_call(
        functools.partial(decode_kernel, parts, steps),
        grid_spec=pltpu.PrefetchScalarGridSpec(
            num_scalar_prefetch=2,
            grid=(heads,),
            in_specs=[
                pl.BlockSpec(pick.shape, lambda h, *_: (0, 0)),
                column(dq.shape[0], group * HD),
                column(dk.shape[0], HD),
                column(dv.shape[0], HD),
                column(ctx, HD),
                column(ctx, HD),
            ],
            out_specs=[
                pl.BlockSpec((parts, None, HD, cols), lambda h, *_: (0, h, 0, 0)),
                pl.BlockSpec((parts, None, 1, cols), lambda h, *_: (0, h, 0, 0)),
            ],
            scratch_shapes=[
                pltpu.VMEM((count, HD), jnp.bfloat16),
                pltpu.VMEM((HD, count), jnp.float32),
                pltpu.VMEM((1, count), jnp.float32),
                pltpu.VMEM((1, count), jnp.float32),
            ],
        ),
        out_shape=[
            jax.ShapeDtypeStruct((parts, heads, HD, cols), jnp.bfloat16),
            jax.ShapeDtypeStruct((parts, heads, 1, cols), jnp.float32),
        ],
        compiler_params=pltpu.CompilerParams(vmem_limit_bytes=VMEM_LIMIT),
        name="decode",
    )(meta, keep, pick, dq, dk, dv, keys, values)


def window_kernel(meta, q_ref, k_ref, out, q_s):
    group = q_ref.shape[1] // HD
    for g in range(group):
        q_s[pl.ds(g * W, W), :] = q_ref[:, pl.ds(g * HD, HD)]
    stretches = k_ref.shape[0] // STRETCH

    def level(c, masked):
        s = dot(k_ref[pl.ds(pl.multiple_of(c * STRETCH, STRETCH), STRETCH), :], q_s[...], NT)
        if masked:
            key_at = lax.broadcasted_iota(jnp.int32, s.shape, 0)
            query_at = lax.broadcasted_iota(jnp.int32, s.shape, 1) % W
            s = jnp.where((key_at <= STRETCH - W + query_at) | (meta[1] == 0), s, FILL)
        m = jnp.max(s, axis=0, keepdims=True)
        total = jnp.sum(jnp.exp2(s * SCALE - m * SCALE), axis=0, keepdims=True)
        out[pl.ds(c, 1), :] = m * SCALE + jnp.log2(total)

    def one(c, carry):
        level(c, False)
        return carry

    lax.fori_loop(0, stretches - 1, one, 0)
    level(stretches - 1, True)


def window(meta, queries, keys, heads):
    width = queries.shape[1] // heads
    stretches = keys.shape[0] // STRETCH
    count = W * (width // HD)
    return pl.pallas_call(
        window_kernel,
        grid_spec=pltpu.PrefetchScalarGridSpec(
            num_scalar_prefetch=1,
            grid=(heads,),
            in_specs=[
                pl.BlockSpec((W, width), lambda h, meta: (0, h)),
                pl.BlockSpec((keys.shape[0], HD), lambda h, meta: (0, meta[2] + h)),
            ],
            out_specs=pl.BlockSpec((None, stretches, count), lambda h, meta: (h, 0, 0)),
            scratch_shapes=[pltpu.VMEM((count, HD), jnp.bfloat16)],
        ),
        out_shape=jax.ShapeDtypeStruct((heads, stretches, count), jnp.float32),
        compiler_params=pltpu.CompilerParams(vmem_limit_bytes=VMEM_LIMIT),
        name="window",
    )(meta, queries, keys)


def combine_kernel(part, lse, out):
    parts = part.shape[0]
    top = lse[0]
    for i in range(1, parts):
        top = jnp.maximum(top, lse[i])
    total = jnp.zeros_like(top)
    summed = jnp.zeros(part.shape[1:], jnp.float32)
    for i in range(parts):
        share = jnp.exp2(lse[i] - top)
        total = total + share
        summed = summed + part[i].astype(jnp.float32) * share
    turned = (summed / total).T.astype(jnp.bfloat16)
    per = out.shape[0]
    for g in range(turned.shape[0] // per):
        out[:, pl.ds(g * HD, HD)] = turned[g * per:(g + 1) * per, :]


def combine(part, lse, per):
    parts, heads, depth, cols = part.shape
    width = cols // per * HD
    return pl.pallas_call(
        combine_kernel,
        grid=(heads,),
        in_specs=[
            pl.BlockSpec((parts, None, depth, cols), lambda h: (0, h, 0, 0)),
            pl.BlockSpec((parts, None, 1, cols), lambda h: (0, h, 0, 0)),
        ],
        out_specs=pl.BlockSpec((per, width), lambda h: (0, h)),
        out_shape=jax.ShapeDtypeStruct((per, heads * width), jnp.bfloat16),
        name="combine",
    )(part, lse)


def local(keys, values, window_q, keep_stretches, dec_q, dec_k, dec_v, row_order):
    parts = lax.axis_size("ctx")
    row_count = lax.axis_size("rows")
    own = lax.axis_index("ctx")
    row = lax.axis_index("rows")
    heads = keys.shape[1] // HD
    score_heads = heads // row_count
    rows, steps, _ = dec_q.shape
    each = rows // (parts * row_count)
    meta = jnp.stack([own, (own == parts - 1).astype(jnp.int32), row * score_heads]).astype(jnp.int32)

    cols = window_q.shape[1] // row_count
    mine = lax.dynamic_slice_in_dim(window_q, row * cols, cols, 1)
    queries = lax.all_gather(mine, "ctx", axis=0, tiled=True)

    order = lax.dynamic_slice_in_dim(row_order.reshape(parts, row_count, each), row, 1, 1)
    wanted = order * steps + jnp.arange(steps, dtype=jnp.int32)[None, :, None]
    pick = (wanted.reshape(-1)[:, None] == jnp.arange(rows * steps, dtype=jnp.int32)[None, :])
    pick = pick.astype(jnp.bfloat16)

    flat = lambda x: x.reshape(rows * steps, x.shape[2])
    part, lse = decode(meta, keep_stretches, pick, flat(dec_q), flat(dec_k), flat(dec_v), keys, values, parts, steps)
    part = lax.all_to_all(part, "ctx", 0, 0, tiled=True)
    lse = lax.all_to_all(lse, "ctx", 0, 0, tiled=True)

    level = window(meta, queries, keys, score_heads)
    top = jnp.max(level, axis=1)
    lower = jnp.log2(jnp.sum(jnp.exp2(level - top[:, None, :]), axis=1)) + top
    everyone = lax.all_gather(lower, "ctx")
    top = jnp.max(everyone, axis=0)
    whole = jnp.log2(jnp.sum(jnp.exp2(everyone - top), axis=0)) + top
    stretch_scores = jnp.sum(jnp.exp2(level - whole[:, None, :]), axis=2)

    decoded = combine(part, lse, steps * each)
    decoded = decoded.reshape(steps, each, -1).transpose(1, 0, 2)
    return stretch_scores, decoded


def solution(mesh):
    placed = (
        P(("groups", "ctx"), "head"),
        P(("groups", "ctx"), "head"),
        P(("groups", "ctx"), "head"),
        P(("groups", "head"), None),
        P("groups", None, "head"),
        P("groups", None, "head"),
        P("groups", None, "head"),
        P("groups"),
    )
    return jax.shard_map(
        local,
        mesh=mesh,
        in_specs=placed,
        out_specs=(
            P(("groups", "head", "rows"), "ctx"),
            P(("groups", "ctx", "rows"), None, "head"),
        ),
        check_vma=False,
    )
```

```python
import functools
import math

import jax
import jax.numpy as jnp
from jax import lax
from jax.experimental import pallas as pl
from jax.experimental.pallas import tpu as pltpu
from jax.sharding import PartitionSpec as P

QH = 64
KVH = 8
HD = 128
STRETCH = 512
W = 32
FILL = -1e30
SCALE = HD ** -0.5 * math.log2(math.e)
NN = (((1,), (0,)), ((), ()))
EXTRA = 16
UNROLL = 2
CHUNK = 512
VMEM_LIMIT = 48 * 1024 * 1024


def dot(a, b, dims):
    return lax.dot_general(a, b, dims, preferred_element_type=jnp.float32)


def decode_kernel(parts, steps, meta, keep, pick, dq, dk, dv, k_ref, v_ref, out, q_rows, q_s, acc, m_s, l_s):
    head = pl.program_id(0)
    group = dq.shape[1] // HD
    per = pick.shape[0] // parts
    cols = group * per
    stretches = k_ref.shape[0] // STRETCH
    base = meta[0] * stretches

    gathered = dot(pick[...], dq[...], NN)
    for d in range(parts):
        for g in range(group):
            q_rows[pl.ds(d * cols + g * per, per), :] = gathered[d * per:(d + 1) * per, g * HD:(g + 1) * HD]
    q_s[...] = q_rows[...].T.astype(jnp.bfloat16)
    acc[...] = jnp.zeros_like(acc)
    m_s[...] = jnp.full_like(m_s, FILL)
    l_s[...] = jnp.zeros_like(l_s)

    wide = math.gcd(CHUNK, parts * cols)
    chunks = parts * cols // wide

    def score(key, d):
        return dot(key, q_s[:, pl.ds(d * wide, wide)], NN)

    def fold(s, turned, d):
        at = pl.ds(d * wide, wide)
        m_old = m_s[:, at]
        m_new = jnp.maximum(m_old, jnp.max(s, axis=0, keepdims=True))
        p = jnp.exp2(s * SCALE - m_new * SCALE)
        shrink = jnp.exp2((m_old - m_new) * SCALE)
        both = dot(turned, p.astype(jnp.bfloat16), NN)
        m_s[:, at] = m_new
        l_s[:, at] = l_s[:, at] * shrink + both[HD:HD + 1]
        acc[:, at] = acc[:, at] * shrink + both[:HD]

    def update(blocks, mask=None):
        work = []
        for key, value in blocks:
            ones = jnp.ones((EXTRA, value.shape[0]), jnp.bfloat16)
            turned = jnp.concatenate([value.T, ones], axis=0)
            work += [(key, turned, d) for d in range(chunks)]
        later = score(work[0][0], work[0][2])
        for at, (_, turned, d) in enumerate(work):
            s = later
            if at + 1 < len(work):
                later = score(work[at + 1][0], work[at + 1][2])
            if mask is not None:
                s = jnp.where(mask(d, s.shape), s, FILL)
            fold(s, turned, d)

    def count(i, found):
        start, many = found
        stretch = keep[head, i] - base
        return (start + (stretch < 0).astype(jnp.int32),
                many + ((stretch >= 0) & (stretch < stretches)).astype(jnp.int32))

    start, many = lax.fori_loop(0, keep.shape[1], count, (jnp.int32(0), jnp.int32(0)))

    def block(i):
        at = pl.ds(pl.multiple_of((keep[head, start + i] - base) * STRETCH, STRETCH), STRETCH)
        return k_ref[at, :], v_ref[at, :]

    def several(i, carry):
        update([block(i * UNROLL + u) for u in range(UNROLL)])
        return carry

    def one(i, carry):
        update([block(i)])
        return carry

    lax.fori_loop(0, many // UNROLL, several, 0)
    lax.fori_loop(many // UNROLL * UNROLL, many, one, 0)

    @pl.when(meta[1] == 1)
    def _():
        tail = pl.ds(k_ref.shape[0] - W, W)
        update([(k_ref[tail, :], v_ref[tail, :])])
        own_k = dot(pick[...], dk[...], NN).astype(jnp.bfloat16)
        own_v = dot(pick[...], dv[...], NN).astype(jnp.bfloat16)
        each = per // steps

        def mask(d, shape):
            key_at = lax.broadcasted_iota(jnp.int32, shape, 0)
            query = lax.broadcasted_iota(jnp.int32, shape, 1) + d * wide
            query_at = query % per
            inside = key_at % per
            return ((key_at // per == query // cols) & (inside % each == query_at % each)
                    & (inside // each <= query_at // each))

        update([(own_k, own_v)], mask)

    l = l_s[...]
    some = l > 0.0
    safe = jnp.where(some, l, 1.0)
    inverse = jnp.where(some, 1.0 / safe, 0.0)
    level = jnp.where(some, m_s[...] * SCALE + jnp.log2(safe), FILL)
    high = level.astype(jnp.bfloat16).astype(jnp.float32)
    middle = (level - high).astype(jnp.bfloat16).astype(jnp.float32)
    low = level - high - middle
    pieces = jnp.concatenate([high, middle, low, jnp.zeros((EXTRA - 3, level.shape[1]), jnp.float32)], axis=0)
    for d in range(parts):
        at = pl.ds(d * cols, cols)
        out[d, :HD] = (acc[:, at] * inverse[:, d * cols:(d + 1) * cols]).astype(jnp.bfloat16)
        out[d, HD:] = pieces[:, d * cols:(d + 1) * cols].astype(jnp.bfloat16)


def decode(meta, keep, pick, dq, dk, dv, keys, values, parts, steps):
    heads = keys.shape[1] // HD
    group = dq.shape[1] // (heads * HD)
    count = pick.shape[0] * group
    cols = count // parts
    ctx = keys.shape[0]
    column = lambda rows, width: pl.BlockSpec((rows, width), lambda h, *_: (0, h))
    return pl.pallas_call(
        functools.partial(decode_kernel, parts, steps),
        grid_spec=pltpu.PrefetchScalarGridSpec(
            num_scalar_prefetch=2,
            grid=(heads,),
            in_specs=[
                pl.BlockSpec(pick.shape, lambda h, *_: (0, 0)),
                column(dq.shape[0], group * HD),
                column(dk.shape[0], HD),
                column(dv.shape[0], HD),
                column(ctx, HD),
                column(ctx, HD),
            ],
            out_specs=pl.BlockSpec((parts, None, HD + EXTRA, cols), lambda h, *_: (0, h, 0, 0)),
            scratch_shapes=[
                pltpu.VMEM((count, HD), jnp.float32),
                pltpu.VMEM((HD, count), jnp.bfloat16),
                pltpu.VMEM((HD, count), jnp.float32),
                pltpu.VMEM((1, count), jnp.float32),
                pltpu.VMEM((1, count), jnp.float32),
            ],
        ),
        out_shape=jax.ShapeDtypeStruct((parts, heads, HD + EXTRA, cols), jnp.bfloat16),
        cost_estimate=pl.CostEstimate(
            flops=2 * count * ctx * heads * HD, bytes_accessed=4 * ctx * heads * HD,
            transcendentals=count * ctx * heads // 2,
        ),
        compiler_params=pltpu.CompilerParams(vmem_limit_bytes=VMEM_LIMIT),
        name="decode",
    )(meta, keep, pick, dq, dk, dv, keys, values)


def window_kernel(meta, q_ref, k_ref, out, q_rows, q_s):
    group = q_ref.shape[1] // HD
    for g in range(group):
        q_rows[pl.ds(g * W, W), :] = q_ref[:, pl.ds(g * HD, HD)].astype(jnp.float32)
    q_s[...] = q_rows[...].T.astype(jnp.bfloat16)
    stretches = k_ref.shape[0] // STRETCH
    several = math.gcd(stretches, 4)

    def score(c):
        return dot(k_ref[pl.ds(pl.multiple_of(c * STRETCH, STRETCH), STRETCH), :], q_s[...], NN)

    def levels(first, last):
        later = score(first)
        for u in range(several):
            s = later
            if u + 1 < several:
                later = score(first + u + 1)
            if last and u + 1 == several:
                key_at = lax.broadcasted_iota(jnp.int32, s.shape, 0)
                query_at = lax.broadcasted_iota(jnp.int32, s.shape, 1) % W
                s = jnp.where((key_at <= STRETCH - W + query_at) | (meta[1] == 0), s, FILL)
            m = jnp.max(s, axis=0, keepdims=True)
            total = jnp.sum(jnp.exp2(s * SCALE - m * SCALE), axis=0, keepdims=True)
            out[pl.ds(first + u, 1), :] = m * SCALE + jnp.log2(total)

    def one(c, carry):
        levels(c * several, False)
        return carry

    lax.fori_loop(0, stretches // several - 1, one, 0)
    levels(stretches - several, True)


def window(meta, queries, keys, heads):
    width = queries.shape[1] // heads
    stretches = keys.shape[0] // STRETCH
    count = W * (width // HD)
    return pl.pallas_call(
        window_kernel,
        grid_spec=pltpu.PrefetchScalarGridSpec(
            num_scalar_prefetch=1,
            grid=(heads,),
            in_specs=[
                pl.BlockSpec((W, width), lambda h, meta: (0, h)),
                pl.BlockSpec((keys.shape[0], HD), lambda h, meta: (0, meta[2] + h)),
            ],
            out_specs=pl.BlockSpec((None, stretches, count), lambda h, meta: (h, 0, 0)),
            scratch_shapes=[pltpu.VMEM((count, HD), jnp.float32), pltpu.VMEM((HD, count), jnp.bfloat16)],
        ),
        out_shape=jax.ShapeDtypeStruct((heads, stretches, count), jnp.float32),
        compiler_params=pltpu.CompilerParams(vmem_limit_bytes=VMEM_LIMIT),
        name="window",
    )(meta, queries, keys)


def combine_kernel(part, out):
    parts = part.shape[0]
    blocks = [part[i].astype(jnp.float32) for i in range(parts)]
    levels = [b[HD:HD + 1] + b[HD + 1:HD + 2] + b[HD + 2:HD + 3] for b in blocks]
    top = levels[0]
    for level in levels[1:]:
        top = jnp.maximum(top, level)
    total = jnp.zeros_like(top)
    summed = jnp.zeros((HD, part.shape[2]), jnp.float32)
    for block, level in zip(blocks, levels):
        share = jnp.exp2(level - top)
        total = total + share
        summed = summed + block[:HD] * share
    turned = (summed / total).T.astype(jnp.bfloat16)
    per = out.shape[0]
    for g in range(turned.shape[0] // per):
        out[:, pl.ds(g * HD, HD)] = turned[g * per:(g + 1) * per, :]


def combine(part, per):
    parts, heads, depth, cols = part.shape
    width = cols // per * HD
    return pl.pallas_call(
        combine_kernel,
        grid=(heads,),
        in_specs=[pl.BlockSpec((parts, None, depth, cols), lambda h: (0, h, 0, 0))],
        out_specs=pl.BlockSpec((per, width), lambda h: (0, h)),
        out_shape=jax.ShapeDtypeStruct((per, heads * width), jnp.bfloat16),
        name="combine",
    )(part)


def others(x, axis):
    count = lax.axis_size(axis)
    return [lax.ppermute(x, axis, [(i, (i + shift) % count) for i in range(count)]) for shift in range(1, count)]


def local(keys, values, window_q, keep_stretches, dec_q, dec_k, dec_v, row_order):
    parts = lax.axis_size("ctx")
    row_count = lax.axis_size("rows")
    own = lax.axis_index("ctx")
    row = lax.axis_index("rows")
    heads = keys.shape[1] // HD
    score_heads = heads // row_count
    rows, steps, _ = dec_q.shape
    each = rows // (parts * row_count)
    meta = jnp.stack([own, (own == parts - 1).astype(jnp.int32), row * score_heads]).astype(jnp.int32)

    cols = window_q.shape[1] // row_count
    mine = lax.dynamic_slice_in_dim(window_q, row * cols, cols, 1)
    shifted = others(mine, "ctx")

    order = lax.dynamic_slice_in_dim(row_order.reshape(parts, row_count, each), row, 1, 1)
    wanted = order * steps + jnp.arange(steps, dtype=jnp.int32)[None, :, None]
    pick = (wanted.reshape(-1)[:, None] == jnp.arange(rows * steps, dtype=jnp.int32)[None, :])
    pick = pick.astype(jnp.bfloat16)

    queries = jnp.zeros((W, cols), mine.dtype)
    for shift, block in enumerate([mine] + shifted):
        at = lax.rem(own + parts - shift, parts) * mine.shape[0]
        queries = lax.dynamic_update_slice_in_dim(queries, block, at, 0)
    queries, pick = lax.optimization_barrier((queries, pick))

    flat = lambda x: x.reshape(rows * steps, x.shape[2])
    part = decode(meta, keep_stretches, pick, flat(dec_q), flat(dec_k), flat(dec_v), keys, values, parts, steps)
    part = lax.all_to_all(part, "ctx", 0, 0, tiled=True)

    level = window(meta, queries, keys, score_heads)
    top = jnp.max(level, axis=1)
    lower = jnp.log2(jnp.sum(jnp.exp2(level - top[:, None, :]), axis=1)) + top
    everyone = [lower] + others(lower, "ctx")
    top = functools.reduce(jnp.maximum, everyone)
    whole = jnp.log2(sum(jnp.exp2(one - top) for one in everyone)) + top
    stretch_scores = jnp.sum(jnp.exp2(level - whole[:, None, :]), axis=2)

    decoded = combine(part, steps * each)
    decoded = decoded.reshape(steps, each, -1).transpose(1, 0, 2)
    return stretch_scores, decoded


def solution(mesh):
    placed = (
        P(("groups", "ctx"), "head"),
        P(("groups", "ctx"), "head"),
        P(("groups", "ctx"), "head"),
        P(("groups", "head"), None),
        P("groups", None, "head"),
        P("groups", None, "head"),
        P("groups", None, "head"),
        P("groups"),
    )
    return jax.shard_map(
        local,
        mesh=mesh,
        in_specs=placed,
        out_specs=(
            P(("groups", "head", "rows"), "ctx"),
            P(("groups", "ctx", "rows"), None, "head"),
        ),
        check_vma=False,
    )
```

```python
import functools
import math

import jax
import jax.numpy as jnp
from jax import lax
from jax.experimental import pallas as pl
from jax.experimental.pallas import tpu as pltpu
from jax.sharding import PartitionSpec as P

QH = 64
KVH = 8
HD = 128
STRETCH = 512
W = 32
FILL = -1e30
SCALE = HD ** -0.5 * math.log2(math.e)
NN = (((1,), (0,)), ((), ()))
EXTRA = 16
UNROLL = (4, 2, 1)
CHUNK = 512
VMEM_LIMIT = 48 * 1024 * 1024


def dot(a, b, dims):
    return lax.dot_general(a, b, dims, preferred_element_type=jnp.float32)


def scaled_pieces(q_rows, q_s):
    turned = q_rows[...].T * SCALE
    high = turned.astype(jnp.bfloat16)
    q_s[:HD] = high
    q_s[HD:] = (turned - high.astype(jnp.float32)).astype(jnp.bfloat16)


def twice(key):
    return jnp.concatenate([key, key], axis=1)


def decode_kernel(parts, steps, meta, keep, pick, dq, dk, dv, k_ref, v_ref, out, q_rows, q_s, acc, m_s, l_s):
    head = pl.program_id(0)
    group = dq.shape[1] // HD
    per = pick.shape[0] // parts
    cols = group * per
    stretches = k_ref.shape[0] // STRETCH
    base = meta[0] * stretches

    gathered = dot(pick[...], dq[...], NN)
    for d in range(parts):
        for g in range(group):
            q_rows[pl.ds(d * cols + g * per, per), :] = gathered[d * per:(d + 1) * per, g * HD:(g + 1) * HD]
    scaled_pieces(q_rows, q_s)
    acc[...] = jnp.zeros_like(acc)
    m_s[...] = jnp.full_like(m_s, FILL)
    l_s[...] = jnp.zeros_like(l_s)

    wide = math.gcd(CHUNK, parts * cols)
    chunks = parts * cols // wide

    def score(key, d):
        return dot(key, q_s[:, pl.ds(d * wide, wide)], NN)

    def fold(s, turned, d):
        at = pl.ds(d * wide, wide)
        m_old = m_s[:, at]
        m_new = jnp.maximum(m_old, jnp.max(s, axis=0, keepdims=True))
        p = jnp.exp2(s - m_new)
        shrink = jnp.exp2(m_old - m_new)
        both = dot(turned, p.astype(jnp.bfloat16), NN)
        m_s[:, at] = m_new
        l_s[:, at] = l_s[:, at] * shrink + both[HD:HD + 1]
        acc[:, at] = acc[:, at] * shrink + both[:HD]

    def update(blocks, mask=None):
        work = []
        for key, value in blocks:
            ones = jnp.ones((EXTRA, value.shape[0]), jnp.bfloat16)
            turned = jnp.concatenate([value.T, ones], axis=0)
            work += [(twice(key), turned, d) for d in range(chunks)]
        later = score(work[0][0], work[0][2])
        for at, (_, turned, d) in enumerate(work):
            s = later
            if at + 1 < len(work):
                later = score(work[at + 1][0], work[at + 1][2])
            if mask is not None:
                s = jnp.where(mask(d, s.shape), s, FILL)
            fold(s, turned, d)

    def count(i, found):
        start, many = found
        stretch = keep[head, i] - base
        return (start + (stretch < 0).astype(jnp.int32),
                many + ((stretch >= 0) & (stretch < stretches)).astype(jnp.int32))

    start, many = lax.fori_loop(0, keep.shape[1], count, (jnp.int32(0), jnp.int32(0)))

    def block(i):
        at = pl.ds(pl.multiple_of((keep[head, start + i] - base) * STRETCH, STRETCH), STRETCH)
        return k_ref[at, :], v_ref[at, :]

    done = 0
    for size in UNROLL:
        def several(i, carry, size=size, done=done):
            update([block(done + i * size + u) for u in range(size)])
            return carry

        times = (many - done) // size
        lax.fori_loop(0, times, several, 0)
        done = done + times * size

    @pl.when(meta[1] == 1)
    def _():
        tail = pl.ds(k_ref.shape[0] - W, W)
        update([(k_ref[tail, :], v_ref[tail, :])])
        own_k = dot(pick[...], dk[...], NN).astype(jnp.bfloat16)
        own_v = dot(pick[...], dv[...], NN).astype(jnp.bfloat16)

        def mask(d, shape):
            key_at = lax.broadcasted_iota(jnp.int32, shape, 0)
            query = lax.broadcasted_iota(jnp.int32, shape, 1) + d * wide
            query_at = query % per
            inside = key_at % per
            return ((key_at // per == query // cols) & (inside // steps == query_at // steps)
                    & (inside % steps <= query_at % steps))

        update([(own_k, own_v)], mask)

    l = l_s[...]
    some = l > 0.0
    safe = jnp.where(some, l, 1.0)
    inverse = jnp.where(some, 1.0 / safe, 0.0)
    level = jnp.where(some, m_s[...] + jnp.log2(safe), FILL)
    high = level.astype(jnp.bfloat16).astype(jnp.float32)
    middle = (level - high).astype(jnp.bfloat16).astype(jnp.float32)
    low = level - high - middle
    pieces = jnp.concatenate([high, middle, low, jnp.zeros((EXTRA - 3, level.shape[1]), jnp.float32)], axis=0)
    for d in range(parts):
        at = pl.ds(d * cols, cols)
        out[d, :HD] = (acc[:, at] * inverse[:, d * cols:(d + 1) * cols]).astype(jnp.bfloat16)
        out[d, HD:] = pieces[:, d * cols:(d + 1) * cols].astype(jnp.bfloat16)


def decode(meta, keep, pick, dq, dk, dv, keys, values, parts, steps):
    heads = keys.shape[1] // HD
    group = dq.shape[1] // (heads * HD)
    count = pick.shape[0] * group
    cols = count // parts
    ctx = keys.shape[0]
    column = lambda rows, width: pl.BlockSpec((rows, width), lambda h, *_: (0, h))
    return pl.pallas_call(
        functools.partial(decode_kernel, parts, steps),
        grid_spec=pltpu.PrefetchScalarGridSpec(
            num_scalar_prefetch=2,
            grid=(heads,),
            in_specs=[
                pl.BlockSpec(pick.shape, lambda h, *_: (0, 0)),
                column(dq.shape[0], group * HD),
                column(dk.shape[0], HD),
                column(dv.shape[0], HD),
                column(ctx, HD),
                column(ctx, HD),
            ],
            out_specs=pl.BlockSpec((parts, None, HD + EXTRA, cols), lambda h, *_: (0, h, 0, 0)),
            scratch_shapes=[
                pltpu.VMEM((count, HD), jnp.float32),
                pltpu.VMEM((2 * HD, count), jnp.bfloat16),
                pltpu.VMEM((HD, count), jnp.float32),
                pltpu.VMEM((1, count), jnp.float32),
                pltpu.VMEM((1, count), jnp.float32),
            ],
        ),
        out_shape=jax.ShapeDtypeStruct((parts, heads, HD + EXTRA, cols), jnp.bfloat16),
        cost_estimate=pl.CostEstimate(
            flops=2 * count * ctx * heads * HD, bytes_accessed=4 * ctx * heads * HD,
            transcendentals=count * ctx * heads // 2,
        ),
        compiler_params=pltpu.CompilerParams(vmem_limit_bytes=VMEM_LIMIT),
        name="decode",
    )(meta, keep, pick, dq, dk, dv, keys, values)


def window_kernel(meta, q_ref, k_ref, out, q_rows, q_s):
    group = q_ref.shape[1] // HD
    for g in range(group):
        q_rows[pl.ds(g * W, W), :] = q_ref[:, pl.ds(g * HD, HD)].astype(jnp.float32)
    scaled_pieces(q_rows, q_s)
    stretches = k_ref.shape[0] // STRETCH
    several = math.gcd(stretches, 4)

    def score(c):
        return dot(twice(k_ref[pl.ds(pl.multiple_of(c * STRETCH, STRETCH), STRETCH), :]), q_s[...], NN)

    def levels(first, last):
        later = score(first)
        for u in range(several):
            s = later
            if u + 1 < several:
                later = score(first + u + 1)
            if last and u + 1 == several:
                key_at = lax.broadcasted_iota(jnp.int32, s.shape, 0)
                query_at = lax.broadcasted_iota(jnp.int32, s.shape, 1) % W
                s = jnp.where((key_at <= STRETCH - W + query_at) | (meta[1] == 0), s, FILL)
            m = jnp.max(s, axis=0, keepdims=True)
            total = jnp.sum(jnp.exp2(s - m), axis=0, keepdims=True)
            out[pl.ds(first + u, 1), :] = m + jnp.log2(total)

    def one(c, carry):
        levels(c * several, False)
        return carry

    lax.fori_loop(0, stretches // several - 1, one, 0)
    levels(stretches - several, True)


def window(meta, queries, keys, heads):
    width = queries.shape[1] // heads
    stretches = keys.shape[0] // STRETCH
    count = W * (width // HD)
    return pl.pallas_call(
        window_kernel,
        grid_spec=pltpu.PrefetchScalarGridSpec(
            num_scalar_prefetch=1,
            grid=(heads,),
            in_specs=[
                pl.BlockSpec((W, width), lambda h, meta: (0, h)),
                pl.BlockSpec((keys.shape[0], HD), lambda h, meta: (0, meta[2] + h)),
            ],
            out_specs=pl.BlockSpec((None, stretches, count), lambda h, meta: (h, 0, 0)),
            scratch_shapes=[pltpu.VMEM((count, HD), jnp.float32), pltpu.VMEM((2 * HD, count), jnp.bfloat16)],
        ),
        out_shape=jax.ShapeDtypeStruct((heads, stretches, count), jnp.float32),
        compiler_params=pltpu.CompilerParams(vmem_limit_bytes=VMEM_LIMIT),
        name="window",
    )(meta, queries, keys)


def combine_kernel(part, out):
    parts, heads = part.shape[:2]
    each, steps, columns = out.shape
    width = columns // heads
    for h in range(heads):
        blocks = [part[i, h].astype(jnp.float32) for i in range(parts)]
        levels = [b[HD:HD + 1] + b[HD + 1:HD + 2] + b[HD + 2:HD + 3] for b in blocks]
        top = functools.reduce(jnp.maximum, levels)
        total = jnp.zeros_like(top)
        summed = jnp.zeros((HD, part.shape[3]), jnp.float32)
        for block, level in zip(blocks, levels):
            share = jnp.exp2(level - top)
            total = total + share
            summed = summed + block[:HD] * share
        turned = (summed / total).T
        for g in range(width // HD):
            rows = turned[g * each * steps:(g + 1) * each * steps]
            out[:, :, pl.ds(h * width + g * HD, HD)] = rows.reshape(each, steps, HD).astype(jnp.bfloat16)


def combine(part, steps, each):
    heads, cols = part.shape[1], part.shape[3]
    whole = pl.BlockSpec(memory_space=pltpu.VMEM)
    return pl.pallas_call(
        combine_kernel,
        in_specs=[whole],
        out_specs=whole,
        out_shape=jax.ShapeDtypeStruct((each, steps, heads * cols // (steps * each) * HD), jnp.bfloat16),
        compiler_params=pltpu.CompilerParams(vmem_limit_bytes=16 * 1024 * 1024),
        name="combine",
    )(part)


def others(x, axis):
    count = lax.axis_size(axis)
    return [lax.ppermute(x, axis, [(i, (i + shift) % count) for i in range(count)]) for shift in range(1, count)]


def local(keys, values, window_q, keep_stretches, dec_q, dec_k, dec_v, row_order):
    parts = lax.axis_size("ctx")
    row_count = lax.axis_size("rows")
    own = lax.axis_index("ctx")
    row = lax.axis_index("rows")
    heads = keys.shape[1] // HD
    score_heads = heads // row_count
    rows, steps, _ = dec_q.shape
    each = rows // (parts * row_count)
    meta = jnp.stack([own, (own == parts - 1).astype(jnp.int32), row * score_heads]).astype(jnp.int32)

    cols = window_q.shape[1] // row_count
    mine = lax.dynamic_slice_in_dim(window_q, row * cols, cols, 1)
    shifted = others(mine, "ctx")

    order = lax.dynamic_slice_in_dim(row_order.reshape(parts, row_count, each), row, 1, 1)
    wanted = order.reshape(parts, each, 1) * steps + jnp.arange(steps, dtype=jnp.int32)
    pick = (wanted.reshape(-1)[:, None] == jnp.arange(rows * steps, dtype=jnp.int32)[None, :])
    pick = pick.astype(jnp.bfloat16)

    queries = jnp.zeros((W, cols), mine.dtype)
    for shift, block in enumerate([mine] + shifted):
        at = lax.rem(own + parts - shift, parts) * mine.shape[0]
        queries = lax.dynamic_update_slice_in_dim(queries, block, at, 0)
    queries, pick = lax.optimization_barrier((queries, pick))

    flat = lambda x: x.reshape(rows * steps, x.shape[2])
    part = decode(meta, keep_stretches, pick, flat(dec_q), flat(dec_k), flat(dec_v), keys, values, parts, steps)
    part = lax.all_to_all(part, "ctx", 0, 0, tiled=True)

    level = window(meta, queries, keys, score_heads)
    top = jnp.max(level, axis=1)
    lower = jnp.log2(jnp.sum(jnp.exp2(level - top[:, None, :]), axis=1)) + top
    everyone = [lower] + others(lower, "ctx")
    top = functools.reduce(jnp.maximum, everyone)
    whole = jnp.log2(sum(jnp.exp2(one - top) for one in everyone)) + top
    stretch_scores = jnp.sum(jnp.exp2(level - whole[:, None, :]), axis=2)

    decoded = combine(part, steps, each)
    return stretch_scores, decoded


def solution(mesh):
    placed = (
        P(("groups", "ctx"), "head"),
        P(("groups", "ctx"), "head"),
        P(("groups", "ctx"), "head"),
        P(("groups", "head"), None),
        P("groups", None, "head"),
        P("groups", None, "head"),
        P("groups", None, "head"),
        P("groups"),
    )
    return jax.shard_map(
        local,
        mesh=mesh,
        in_specs=placed,
        out_specs=(
            P(("groups", "head", "rows"), "ctx"),
            P(("groups", "ctx", "rows"), None, "head"),
        ),
        check_vma=False,
    )
```

```python
import functools
import math

import jax
import jax.numpy as jnp
from jax import lax
from jax.experimental import pallas as pl
from jax.experimental.pallas import tpu as pltpu
from jax.sharding import PartitionSpec as P

QH = 64
KVH = 8
HD = 128
STRETCH = 512
W = 32
FILL = -1e30
SCALE = HD ** -0.5 * math.log2(math.e)
NN = (((1,), (0,)), ((), ()))
EXTRA = 16
UNROLL = (8, 4, 2, 1)
CHUNK = 512
VMEM_LIMIT = 48 * 1024 * 1024


def dot(a, b, dims):
    return lax.dot_general(a, b, dims, preferred_element_type=jnp.float32)


def scaled_pieces(q_rows, q_s):
    turned = q_rows[...].T * SCALE
    high = turned.astype(jnp.bfloat16)
    q_s[:HD] = high
    q_s[HD:] = (turned - high.astype(jnp.float32)).astype(jnp.bfloat16)


def twice(key):
    return jnp.concatenate([key, key], axis=1)


def decode_kernel(parts, steps, meta, keep, pick, dq, dk, dv, k_ref, v_ref, out, q_rows, q_s, acc, m_s, l_s):
    head = pl.program_id(0)
    group = dq.shape[1] // HD
    per = pick.shape[0] // parts
    cols = group * per
    stretches = k_ref.shape[0] // STRETCH
    base = meta[0] * stretches

    gathered = dot(pick[...], dq[...], NN)
    for d in range(parts):
        for g in range(group):
            q_rows[pl.ds(d * cols + g * per, per), :] = gathered[d * per:(d + 1) * per, g * HD:(g + 1) * HD]
    scaled_pieces(q_rows, q_s)
    acc[...] = jnp.zeros_like(acc)
    m_s[...] = jnp.full_like(m_s, FILL)
    l_s[...] = jnp.zeros_like(l_s)

    wide = math.gcd(CHUNK, parts * cols)
    chunks = parts * cols // wide

    def score(key, d):
        return dot(key, q_s[:, pl.ds(d * wide, wide)], NN)

    def fold(s, turned, d):
        at = pl.ds(d * wide, wide)
        m_old = m_s[:, at]
        m_new = jnp.maximum(m_old, jnp.max(s, axis=0, keepdims=True))
        p = jnp.exp2(s - m_new)
        shrink = jnp.exp2(m_old - m_new)
        both = dot(turned, p.astype(jnp.bfloat16), NN)
        m_s[:, at] = m_new
        l_s[:, at] = l_s[:, at] * shrink + both[HD:HD + 1]
        acc[:, at] = acc[:, at] * shrink + both[:HD]

    def update(blocks, mask=None):
        work = []
        for key, value in blocks:
            ones = jnp.ones((EXTRA, value.shape[0]), jnp.bfloat16)
            turned = jnp.concatenate([value.T, ones], axis=0)
            work += [(twice(key), turned, d) for d in range(chunks)]
        later = score(work[0][0], work[0][2])
        for at, (_, turned, d) in enumerate(work):
            s = later
            if at + 1 < len(work):
                later = score(work[at + 1][0], work[at + 1][2])
            if mask is not None:
                s = jnp.where(mask(d, s.shape), s, FILL)
            fold(s, turned, d)

    def count(i, found):
        start, many = found
        stretch = keep[head, i] - base
        return (start + (stretch < 0).astype(jnp.int32),
                many + ((stretch >= 0) & (stretch < stretches)).astype(jnp.int32))

    start, many = lax.fori_loop(0, keep.shape[1], count, (jnp.int32(0), jnp.int32(0)))

    def block(i):
        at = pl.ds(pl.multiple_of((keep[head, start + i] - base) * STRETCH, STRETCH), STRETCH)
        return k_ref[at, :], v_ref[at, :]

    done = 0
    for size in UNROLL:
        def several(i, carry, size=size, done=done):
            update([block(done + i * size + u) for u in range(size)])
            return carry

        times = (many - done) // size
        lax.fori_loop(0, times, several, 0)
        done = done + times * size

    @pl.when(meta[1] == 1)
    def _():
        tail = pl.ds(k_ref.shape[0] - W, W)
        update([(k_ref[tail, :], v_ref[tail, :])])
        own_k = dot(pick[...], dk[...], NN).astype(jnp.bfloat16)
        own_v = dot(pick[...], dv[...], NN).astype(jnp.bfloat16)

        def mask(d, shape):
            key_at = lax.broadcasted_iota(jnp.int32, shape, 0)
            query = lax.broadcasted_iota(jnp.int32, shape, 1) + d * wide
            query_at = query % per
            inside = key_at % per
            return ((key_at // per == query // cols) & (inside // steps == query_at // steps)
                    & (inside % steps <= query_at % steps))

        update([(own_k, own_v)], mask)

    l = l_s[...]
    some = l > 0.0
    safe = jnp.where(some, l, 1.0)
    inverse = jnp.where(some, 1.0 / safe, 0.0)
    level = jnp.where(some, m_s[...] + jnp.log2(safe), FILL)
    high = level.astype(jnp.bfloat16).astype(jnp.float32)
    middle = (level - high).astype(jnp.bfloat16).astype(jnp.float32)
    low = level - high - middle
    pieces = jnp.concatenate([high, middle, low, jnp.zeros((EXTRA - 3, level.shape[1]), jnp.float32)], axis=0)
    for d in range(parts):
        at = pl.ds(d * cols, cols)
        out[d, :HD] = (acc[:, at] * inverse[:, d * cols:(d + 1) * cols]).astype(jnp.bfloat16)
        out[d, HD:] = pieces[:, d * cols:(d + 1) * cols].astype(jnp.bfloat16)


def decode(meta, keep, pick, dq, dk, dv, keys, values, parts, steps):
    heads = keys.shape[1] // HD
    group = dq.shape[1] // (heads * HD)
    count = pick.shape[0] * group
    cols = count // parts
    ctx = keys.shape[0]
    column = lambda rows, width: pl.BlockSpec((rows, width), lambda h, *_: (0, h))
    return pl.pallas_call(
        functools.partial(decode_kernel, parts, steps),
        grid_spec=pltpu.PrefetchScalarGridSpec(
            num_scalar_prefetch=2,
            grid=(heads,),
            in_specs=[
                pl.BlockSpec(pick.shape, lambda h, *_: (0, 0)),
                column(dq.shape[0], group * HD),
                column(dk.shape[0], HD),
                column(dv.shape[0], HD),
                column(ctx, HD),
                column(ctx, HD),
            ],
            out_specs=pl.BlockSpec((parts, None, HD + EXTRA, cols), lambda h, *_: (0, h, 0, 0)),
            scratch_shapes=[
                pltpu.VMEM((count, HD), jnp.float32),
                pltpu.VMEM((2 * HD, count), jnp.bfloat16),
                pltpu.VMEM((HD, count), jnp.float32),
                pltpu.VMEM((1, count), jnp.float32),
                pltpu.VMEM((1, count), jnp.float32),
            ],
        ),
        out_shape=jax.ShapeDtypeStruct((parts, heads, HD + EXTRA, cols), jnp.bfloat16),
        cost_estimate=pl.CostEstimate(
            flops=2 * count * ctx * heads * HD, bytes_accessed=4 * ctx * heads * HD,
            transcendentals=count * ctx * heads // 2,
        ),
        compiler_params=pltpu.CompilerParams(vmem_limit_bytes=VMEM_LIMIT),
        name="decode",
    )(meta, keep, pick, dq, dk, dv, keys, values)


def window_kernel(meta, q_ref, k_ref, out, q_rows, q_s):
    group = q_ref.shape[1] // HD
    for g in range(group):
        q_rows[pl.ds(g * W, W), :] = q_ref[:, pl.ds(g * HD, HD)].astype(jnp.float32)
    scaled_pieces(q_rows, q_s)
    stretches = k_ref.shape[0] // STRETCH
    several = math.gcd(stretches, 4)

    def score(c):
        return dot(twice(k_ref[pl.ds(pl.multiple_of(c * STRETCH, STRETCH), STRETCH), :]), q_s[...], NN)

    def levels(first, last):
        later = score(first)
        for u in range(several):
            s = later
            if u + 1 < several:
                later = score(first + u + 1)
            if last and u + 1 == several:
                key_at = lax.broadcasted_iota(jnp.int32, s.shape, 0)
                query_at = lax.broadcasted_iota(jnp.int32, s.shape, 1) % W
                s = jnp.where((key_at <= STRETCH - W + query_at) | (meta[1] == 0), s, FILL)
            m = jnp.max(s, axis=0, keepdims=True)
            total = jnp.sum(jnp.exp2(s - m), axis=0, keepdims=True)
            out[pl.ds(first + u, 1), :] = m + jnp.log2(total)

    def one(c, carry):
        levels(c * several, False)
        return carry

    lax.fori_loop(0, stretches // several - 1, one, 0)
    levels(stretches - several, True)


def window(meta, queries, keys, heads):
    width = queries.shape[1] // heads
    stretches = keys.shape[0] // STRETCH
    count = W * (width // HD)
    return pl.pallas_call(
        window_kernel,
        grid_spec=pltpu.PrefetchScalarGridSpec(
            num_scalar_prefetch=1,
            grid=(heads,),
            in_specs=[
                pl.BlockSpec((W, width), lambda h, meta: (0, h)),
                pl.BlockSpec((keys.shape[0], HD), lambda h, meta: (0, meta[2] + h)),
            ],
            out_specs=pl.BlockSpec((None, stretches, count), lambda h, meta: (h, 0, 0)),
            scratch_shapes=[pltpu.VMEM((count, HD), jnp.float32), pltpu.VMEM((2 * HD, count), jnp.bfloat16)],
        ),
        out_shape=jax.ShapeDtypeStruct((heads, stretches, count), jnp.float32),
        compiler_params=pltpu.CompilerParams(vmem_limit_bytes=VMEM_LIMIT),
        name="window",
    )(meta, queries, keys)


def combine_kernel(part, out):
    parts, heads = part.shape[:2]
    each, steps, columns = out.shape
    width = columns // heads
    for h in range(heads):
        blocks = [part[i, h].astype(jnp.float32) for i in range(parts)]
        levels = [b[HD:HD + 1] + b[HD + 1:HD + 2] + b[HD + 2:HD + 3] for b in blocks]
        top = functools.reduce(jnp.maximum, levels)
        total = jnp.zeros_like(top)
        summed = jnp.zeros((HD, part.shape[3]), jnp.float32)
        for block, level in zip(blocks, levels):
            share = jnp.exp2(level - top)
            total = total + share
            summed = summed + block[:HD] * share
        turned = (summed / total).T
        for g in range(width // HD):
            rows = turned[g * each * steps:(g + 1) * each * steps]
            out[:, :, pl.ds(h * width + g * HD, HD)] = rows.reshape(each, steps, HD).astype(jnp.bfloat16)


def combine(part, steps, each):
    heads, cols = part.shape[1], part.shape[3]
    whole = pl.BlockSpec(memory_space=pltpu.VMEM)
    return pl.pallas_call(
        combine_kernel,
        in_specs=[whole],
        out_specs=whole,
        out_shape=jax.ShapeDtypeStruct((each, steps, heads * cols // (steps * each) * HD), jnp.bfloat16),
        compiler_params=pltpu.CompilerParams(vmem_limit_bytes=16 * 1024 * 1024),
        name="combine",
    )(part)


def others(x, axis):
    count = lax.axis_size(axis)
    return [lax.ppermute(x, axis, [(i, (i + shift) % count) for i in range(count)]) for shift in range(1, count)]


def local(keys, values, window_q, keep_stretches, dec_q, dec_k, dec_v, row_order):
    parts = lax.axis_size("ctx")
    row_count = lax.axis_size("rows")
    own = lax.axis_index("ctx")
    row = lax.axis_index("rows")
    heads = keys.shape[1] // HD
    score_heads = heads // row_count
    rows, steps, _ = dec_q.shape
    each = rows // (parts * row_count)
    meta = jnp.stack([own, (own == parts - 1).astype(jnp.int32), row * score_heads]).astype(jnp.int32)

    cols = window_q.shape[1] // row_count
    mine = lax.dynamic_slice_in_dim(window_q, row * cols, cols, 1)
    shifted = others(mine, "ctx")

    order = lax.dynamic_slice_in_dim(row_order.reshape(parts, row_count, each), row, 1, 1)
    wanted = order.reshape(parts, each, 1) * steps + jnp.arange(steps, dtype=jnp.int32)
    pick = (wanted.reshape(-1)[:, None] == jnp.arange(rows * steps, dtype=jnp.int32)[None, :])
    pick = pick.astype(jnp.bfloat16)

    queries = jnp.zeros((W, cols), mine.dtype)
    for shift, block in enumerate([mine] + shifted):
        at = lax.rem(own + parts - shift, parts) * mine.shape[0]
        queries = lax.dynamic_update_slice_in_dim(queries, block, at, 0)
    queries, pick = lax.optimization_barrier((queries, pick))

    flat = lambda x: x.reshape(rows * steps, x.shape[2])
    part = decode(meta, keep_stretches, pick, flat(dec_q), flat(dec_k), flat(dec_v), keys, values, parts, steps)
    part = lax.all_to_all(part, "ctx", 0, 0, tiled=True)

    level = window(meta, queries, keys, score_heads)
    top = jnp.max(level, axis=1)
    lower = jnp.log2(jnp.sum(jnp.exp2(level - top[:, None, :]), axis=1)) + top
    everyone = [lower] + others(lower, "ctx")
    top = functools.reduce(jnp.maximum, everyone)
    whole = jnp.log2(sum(jnp.exp2(one - top) for one in everyone)) + top
    stretch_scores = jnp.sum(jnp.exp2(level - whole[:, None, :]), axis=2)

    decoded = combine(part, steps, each)
    return stretch_scores, decoded


def solution(mesh):
    placed = (
        P(("groups", "ctx"), "head"),
        P(("groups", "ctx"), "head"),
        P(("groups", "ctx"), "head"),
        P(("groups", "head"), None),
        P("groups", None, "head"),
        P("groups", None, "head"),
        P("groups", None, "head"),
        P("groups"),
    )
    return jax.shard_map(
        local,
        mesh=mesh,
        in_specs=placed,
        out_specs=(
            P(("groups", "head", "rows"), "ctx"),
            P(("groups", "ctx", "rows"), None, "head"),
        ),
        check_vma=False,
    )
```
